512 devices in a mesh: rep: 32 (over y_lo, z), fsdp: 16 (over y_hi, x, core).
Axes of the slice: x: 4, y: 8 (y_hi: 2, y_lo: 4; y = y_hi * 4 + y_lo), z: 8, core: 2. Of those that a mesh axis runs over, the one named last changes fastest.
Arguments:
- activations: bfloat16 [32, 3072, 4096], P('rep', 'fsdp'), may hold values from -6 to 6
- cotangent: bfloat16 [32, 3072, 2048], P('rep', 'fsdp'), may hold values from -6 to 6
- local_weights: bfloat16 [32, 4096, 2048], P('rep', 'fsdp'), may hold values from -3 to 3
- base_shard: float32 [16, 256, 2048], P('fsdp', 'rep'), may hold values from -6 to 6
- momentum: float32 [16, 256, 2048], P('fsdp', 'rep'), may hold values from -3 to 3
Outputs:
- new_base: float32 [16, 256, 2048], P('fsdp', 'rep')
- new_moment: float32 [16, 256, 2048], P('fsdp', 'rep')
The draws below stay inside these ranges and needn't reach their ends.
All inputs are finite; a program needn't handle non-finite values.
Results may differ from the reference program's by a relative error of at most 0.0095.
Values may be sent and summed in bfloat16 or wider, within the bound.
No kernel may reach another device: no remote copies, remote signals or barrier semaphores. Data moves between devices by JAX's collectives and lax.ppermute only.
A program may use at most 64 MiB of HBM per device.

```python
import math
import jax
import jax.numpy as jnp
from jax import lax

D = 4096
KV = 1024
RTOK = 3072
N_REP = 32
N_FSDP = 16


def steps_of(rng, shape, shards, low, top_value):
    loudness, own = 1.0, jax.random.fold_in(rng, 6)
    for dim, blocks in shards:
        heights = jnp.exp(jax.random.uniform(jax.random.fold_in(own, dim), (blocks,), jnp.float32, low / len(shards), top_value / len(shards)))
        loudness = loudness * jnp.repeat(heights, shape[dim] // blocks).reshape([-1 if axis == dim else 1 for axis in range(len(shape))])
    return loudness


def noise(stream_key, shape, spread, most, shards=(), kind=jnp.bfloat16):
    gain = steps_of(stream_key, shape, shards, -0.22, 0.18) if shards else 1.0
    values = jax.random.normal(stream_key, shape, jnp.float32) * spread * gain
    return jnp.minimum(jnp.maximum(values, -most), most).astype(kind)


def setup_inputs(seed: int = 0) -> dict:
    key_of = jax.random.split(jax.random.key(seed), 6)
    return {
        "activations": noise(key_of[0], (N_REP, RTOK, D), 1.0, 6.0, ((0, 32), (1, 16))),
        "cotangent": noise(key_of[1], (N_REP, RTOK, 2 * KV), 1.0, 6.0, ((0, 32), (1, 16))),
        "local_weights": noise(key_of[2], (N_REP, D, 2 * KV), 0.5, 3.0, ((0, 32), (1, 16))),
        "base_shard": noise(key_of[3], (N_FSDP, D // N_FSDP, 2 * KV), 1.0, 6.0, ((0, 16), (1, 32)), jnp.float32),
        "momentum": noise(key_of[4], (N_FSDP, D // N_FSDP, 2 * KV), 0.5, 3.0, ((0, 16), (1, 32)), jnp.float32),
    }


MOMENTUM_RATE = 0.9
OUTER_RATE = 0.7
EPSILON = 1e-06
TWO_PI = 2.0 * math.pi

def quantize(pseudo_grad):
    height, width = pseudo_grad.shape
    blocks = pseudo_grad.reshape(height, width // 128, 128)
    block_scale = (lax.optimization_barrier(jnp.max(jnp.abs(blocks), axis=2)) + EPSILON).astype(jnp.bfloat16)
    held_scale = lax.optimization_barrier(block_scale)
    level = 7.0 * (blocks / held_scale.astype(jnp.float32)[:, :, None])
    stair = level - jnp.sin(TWO_PI * level) / TWO_PI
    code_values = stair.astype(jnp.bfloat16)
    return (code_values, block_scale)

def restore(code_values, block_scale):
    return code_values.astype(jnp.float32) * (block_scale.astype(jnp.float32) / 7.0)[..., None]

def reference(activations, cotangent, local_weights, base_shard, momentum):
    width = 2 * KV
    base_rows = base_shard.reshape(D, width)
    inverse_root = 1.0 / math.sqrt(RTOK)

    def one_replica(running, replica):
        features, cotan_rows, weights = replica
        gradient = jnp.dot(features.T, cotan_rows, preferred_element_type=jnp.float32)
        pseudo_grad = base_rows - (weights.astype(jnp.float32) - gradient * inverse_root)
        code_values, block_scale = quantize(pseudo_grad)
        return (running + restore(code_values, block_scale).reshape(D, width), None)
    summed, _ = lax.scan(one_replica, jnp.zeros((D, width), jnp.float32), (activations, cotangent, local_weights))
    average = (summed / N_REP).reshape(base_shard.shape)
    new_moment = MOMENTUM_RATE * momentum + average
    new_base = base_shard - OUTER_RATE * (average + MOMENTUM_RATE * new_moment)
    return (new_base, new_moment)
```

```python
import math

import jax
import jax.numpy as jnp
from jax import lax
from jax.experimental import pallas as pl
from jax.experimental.pallas import tpu as pltpu
from jax.sharding import Mesh, PartitionSpec as P

MOMENTUM_RATE = 0.9
OUTER_RATE = 0.7
EPSILON = 1e-06
SINE = (6.57973575592041, -12.987845420837402, 12.207462310791016, -6.687273025512695, 2.36698842048645, -0.5099183320999146)
REP = ("ylo", "z")
PEERS = ("ylo", "z", "c")
X, YLO, Z = 4, 4, 8
N_REP = YLO * Z
TOK, D, W2 = 192, 4096, 2048
HALF = W2 // 2
ROWS = 512
INV = 1.0 / math.sqrt(TOK * 16)


def shift(size, k):
    return [(i, (i + k) % size) for i in range(size)]


def matmul_kernel(*refs):
    a_refs, c_refs, out_ref, a_all, c_all, sems = refs[:8], refs[8:12], refs[12], refs[13], refs[14], refs[15]
    copies = []
    for k in range(X):
        copies.append(pltpu.make_async_copy(c_refs[k], c_all.at[pl.ds(k * 384, 384)], sems.at[k]))
        copies.append(pltpu.make_async_copy(a_refs[k], a_all.at[pl.ds(k * 384, 192)], sems.at[4 + k]))
        copies.append(pltpu.make_async_copy(a_refs[4 + k], a_all.at[pl.ds(k * 384 + 192, 192)], sems.at[8 + k]))
    for c in copies:
        c.start()
    for c in copies:
        c.wait()
    for m in range(2):
        part = lax.dot_general(
            a_all[:, m * 256:(m + 1) * 256], c_all[...], (((0,), (0,)), ((), ())),
            preferred_element_type=jnp.float32)
        out_ref[m * 256:(m + 1) * 256, :] = (part * INV).astype(out_ref.dtype)


def matmul(a, c, dtype):
    return pl.pallas_call(
        matmul_kernel,
        out_shape=jax.ShapeDtypeStruct((ROWS, HALF), dtype),
        in_specs=[pl.BlockSpec(memory_space=pl.ANY)] * 12,
        out_specs=pl.BlockSpec(memory_space=pltpu.VMEM),
        scratch_shapes=[
            pltpu.VMEM((1536, ROWS), jnp.bfloat16),
            pltpu.VMEM((1536, HALF), jnp.bfloat16),
            pltpu.SemaphoreType.DMA((12,)),
        ],
        compiler_params=pltpu.CompilerParams(vmem_limit_bytes=40 * 1024 * 1024),
        cost_estimate=pl.CostEstimate(flops=2 * 1536 * ROWS * HALF, bytes_accessed=7 << 20, transcendentals=0),
    )(*a, *c)


def quantize_kernel(own_ref, part_ref, local_ref, base_ref, out_ref):
    rows = own_ref.shape[0]
    pairs = rows // 8
    for j in range(0, 8, 2):
        restored = []
        for col in (j, j + 1):
            lanes = slice(col * 128, (col + 1) * 128)
            gradient = own_ref[:, lanes] + part_ref[:, lanes].astype(jnp.float32)
            base = base_ref[:, 0, col * 8:(col + 1) * 8, :].reshape(rows, 128)
            pseudo = base - (local_ref[:, lanes].astype(jnp.float32) - gradient)
            scale = (jnp.max(jnp.abs(pseudo), axis=1, keepdims=True) + EPSILON).astype(jnp.bfloat16).astype(jnp.float32)
            level = pseudo * (7.0 / scale)
            step = jnp.round(level)
            off = level - step
            square = off * off
            poly = SINE[-1]
            for coef in SINE[-2::-1]:
                poly = poly * square + coef
            code = (step + off * square * poly).astype(jnp.bfloat16).astype(jnp.float32)
            restored.append((code * (scale * (1.0 / 7.0))).reshape(pairs, 8, 128))
        out_ref[:, 0, j * 8:(j + 2) * 8, :] = jnp.concatenate(restored, axis=1).astype(jnp.bfloat16)


def quantize(own, part, local, base):
    rows = 64
    steps = 256 // rows
    tile = pl.BlockSpec((rows, HALF), lambda c, i: (c * steps + i, 0))
    blocks = pl.BlockSpec((rows // 8, 1, 64, 128), lambda c, i: (i, c, 0, 0))
    return pl.pallas_call(
        quantize_kernel,
        grid=(2, steps),
        out_shape=jax.ShapeDtypeStruct((N_REP, 2, 64, 128), jnp.bfloat16),
        in_specs=[tile, tile, tile, blocks],
        out_specs=blocks,
        compiler_params=pltpu.CompilerParams(vmem_limit_bytes=32 * 1024 * 1024),
        cost_estimate=pl.CostEstimate(flops=30 * ROWS * HALF, bytes_accessed=6 << 20, transcendentals=0),
    )(own, part, local, base)


def outer_kernel(got_ref, base_ref, moment_ref, new_base_ref, new_moment_ref):
    for c in range(2):
        total = jnp.sum(got_ref[:, c].astype(jnp.float32), axis=0)
        for j in range(8):
            lanes = slice(c * HALF + j * 128, c * HALF + (j + 1) * 128)
            average = total[j * 8:(j + 1) * 8] / N_REP
            moment = MOMENTUM_RATE * moment_ref[:, lanes] + average
            new_moment_ref[:, lanes] = moment
            new_base_ref[:, lanes] = base_ref[:, lanes] - OUTER_RATE * (average + MOMENTUM_RATE * moment)


def outer(got, base, moment):
    shape = jax.ShapeDtypeStruct(base.shape, jnp.float32)
    return pl.pallas_call(
        outer_kernel,
        out_shape=(shape, shape),
        compiler_params=pltpu.CompilerParams(vmem_limit_bytes=32 * 1024 * 1024),
        cost_estimate=pl.CostEstimate(flops=2 << 20, bytes_accessed=2 << 20, transcendentals=0),
    )(got, base, moment)


def body(activations, cotangent, local_weights, base_shard, momentum):
    x, yhi, c = lax.axis_index("x"), lax.axis_index("yhi"), lax.axis_index("c")
    act, cot, local, base, moment = activations[0], cotangent[0], local_weights[0], base_shard[0], momentum[0]

    def columns(array, index, width):
        return lax.dynamic_slice_in_dim(array, index * width, width, 1)

    def other_core(array):
        return lax.ppermute(array, "c", shift(2, 1))

    mine = columns(cot, c, HALF)
    pair = jnp.concatenate([mine, other_core(columns(cot, 1 - c, HALF))])
    c_parts = [pair] + [lax.ppermute(pair, "x", shift(X, k)) for k in range(1, X)]

    def features(half):
        own = [columns(act, half * X + lax.rem(x + k, X), ROWS) for k in range(X)]
        own = [own[0]] + [lax.ppermute(own[k], "x", shift(X, k)) for k in range(1, X)]
        return own + [other_core(a) for a in own]

    far = matmul(features(1 - yhi), c_parts, jnp.bfloat16)
    far = lax.ppermute(far, "yhi", shift(2, 1))
    near = matmul(features(yhi), c_parts, jnp.float32)

    local_mine, local_other = columns(local, c, HALF), other_core(columns(local, 1 - c, HALF))
    local_rows = jnp.concatenate([jnp.where(c == 0, local_mine, local_other), jnp.where(c == 0, local_other, local_mine)])

    sent = base.reshape(8, 2, 8, 128).transpose(1, 2, 0, 3).reshape(2, 64, 128)
    sent = jnp.broadcast_to(sent[None], (N_REP, 2, 64, 128)).reshape(2 * N_REP, 64, 128)
    base_rows = lax.all_to_all(sent, PEERS, 0, 0, tiled=True).reshape(N_REP, 2, 64, 128)

    restored = quantize(near, far, local_rows, base_rows)
    got = lax.all_to_all(restored.reshape(2 * N_REP, 64, 128), PEERS, 0, 0, tiled=True)
    new_base, new_moment = outer(got.reshape(N_REP, 2, 64, 128), base, moment)
    return new_base[None], new_moment[None]


def solution(mesh):
    fine = Mesh(mesh.devices.reshape(YLO, Z, 2, X, 2), ("ylo", "z", "yhi", "x", "c"))
    rep, fsdp = REP, ("yhi", "x", "c")
    return jax.shard_map(
        body,
        mesh=fine,
        in_specs=(
            P(rep, fsdp, None),
            P(rep, fsdp, None),
            P(rep, fsdp, None),
            P(fsdp, rep, None),
            P(fsdp, rep, None),
        ),
        out_specs=(P(fsdp, rep, None), P(fsdp, rep, None)),
        check_vma=False,
    )
```

```python
import math

import jax
import jax.numpy as jnp
from jax import lax
from jax.experimental import pallas as pl
from jax.experimental.pallas import tpu as pltpu
from jax.sharding import Mesh, PartitionSpec as P

MOMENTUM_RATE = 0.9
OUTER_RATE = 0.7
EPSILON = 1e-06
SINE = (6.57973575592041, -12.987845420837402, 12.207462310791016, -6.687273025512695, 2.36698842048645, -0.5099183320999146)
COST = pl.CostEstimate(flops=1, bytes_accessed=1, transcendentals=0)
REP = ("ylo", "z")
PEERS = ("ylo", "z", "c")
X, YLO, Z = 4, 4, 8
N_REP = YLO * Z
TOK, D, W2 = 192, 4096, 2048
HALF = W2 // 2
CHUNK = HALF // 2
BLOCKS = CHUNK // 128
ROWS = 512
INV = 1.0 / math.sqrt(TOK * 16)


def shift(size, k):
    return [(i, (i + k) % size) for i in range(size)]


def matmul_kernel(*refs):
    others, features, columns, out_ref = refs[:X], refs[X:2 * X], refs[2 * X:3 * X], refs[3 * X]
    a_all, c_all, sems = refs[3 * X + 1:]
    copies = []
    for k in range(X):
        copies.append((others[k], a_all.at[k, 1]))
        copies.append((features[k].at[0], a_all.at[k, 0]))
        copies.append((columns[k].at[1:3], c_all.at[k]))
    copies = [pltpu.make_async_copy(*ends, sems.at[i]) for i, ends in enumerate(copies)]
    for copy in copies:
        copy.start()
    for copy in copies:
        copy.wait()
    everything = c_all[...].reshape(2 * X * TOK, CHUNK)
    for m in range(2):
        rows = slice(m * 256, (m + 1) * 256)
        part = lax.dot_general(
            a_all[:, :, :, rows].reshape(2 * X * TOK, 256), everything, (((0,), (0,)), ((), ())),
            preferred_element_type=jnp.float32)
        out_ref[rows, :] = (part * INV).astype(out_ref.dtype)


def matmul(others, features, columns, dtype):
    return pl.pallas_call(
        matmul_kernel,
        out_shape=jax.ShapeDtypeStruct((ROWS, CHUNK), dtype),
        in_specs=[pl.BlockSpec(memory_space=pl.ANY)] * (3 * X),
        out_specs=pl.BlockSpec(memory_space=pltpu.VMEM),
        scratch_shapes=[
            pltpu.VMEM((X, 2, TOK, ROWS), jnp.bfloat16),
            pltpu.VMEM((X, 2, TOK, CHUNK), jnp.bfloat16),
            pltpu.SemaphoreType.DMA((3 * X,)),
        ],
        compiler_params=pltpu.CompilerParams(vmem_limit_bytes=8 * 1024 * 1024),
        cost_estimate=COST,
    )(*others, *features, *columns)


def quantize_kernel(own_ref, part_ref, local_ref, base_ref, out_ref):
    rows = own_ref.shape[0]
    for j in range(0, BLOCKS, 2):
        restored = []
        for col in (j, j + 1):
            lanes = slice(col * 128, (col + 1) * 128)
            gradient = own_ref[:, lanes] + part_ref[:, lanes].astype(jnp.float32)
            base = base_ref[0, :, 0, :, lanes].reshape(rows, 128)
            pseudo = base - (local_ref[:, lanes].astype(jnp.float32) - gradient)
            scale = (jnp.max(jnp.abs(pseudo), axis=1, keepdims=True) + EPSILON).astype(jnp.bfloat16).astype(jnp.float32)
            level = pseudo * (7.0 / scale)
            step = jnp.round(level)
            off = level - step
            square = off * off
            poly = SINE[-1]
            for coef in SINE[-2::-1]:
                poly = poly * square + coef
            code = (step + off * square * poly).astype(jnp.bfloat16).astype(jnp.float32)
            restored.append((code * (scale * (1.0 / 7.0))).reshape(Z, 8, 128))
        block = jnp.concatenate(restored, axis=1).astype(jnp.bfloat16)
        out_ref[0, :, 0, j * 8:(j + 2) * 8, :] = block


def quantize(own, part, local, base, chunk, earlier=None):
    rows = 8 * Z
    tile = pl.BlockSpec((rows, CHUNK), lambda c, i: (c * YLO + i, 0))
    local_tile = pl.BlockSpec((rows, CHUNK), lambda c, i: (c * YLO + i, chunk))
    out_tile = pl.BlockSpec((1, Z, 1, BLOCKS * 8, 128), lambda c, i: (i, 0, c, chunk, 0))
    base_tile = pl.BlockSpec((1, Z, 1, 8, CHUNK), lambda c, i: (i, 0, c, 0, chunk))
    operands, specs, kernel, aliases = [own, part, local, base], [tile, tile, local_tile, base_tile], quantize_kernel, {}
    if earlier is not None:
        operands.append(earlier)
        specs.append(pl.BlockSpec(memory_space=pl.ANY))
        kernel, aliases = (lambda *refs: quantize_kernel(*refs[:4], refs[5])), {4: 0}
    return pl.pallas_call(
        kernel,
        grid=(2, YLO),
        out_shape=jax.ShapeDtypeStruct((YLO, Z, 2, 2 * BLOCKS * 8, 128), jnp.bfloat16),
        in_specs=specs,
        out_specs=out_tile,
        input_output_aliases=aliases,
        compiler_params=pltpu.CompilerParams(vmem_limit_bytes=5 * 1024 * 1024),
        cost_estimate=COST,
    )(*operands)


def outer_kernel(got_ref, base_ref, moment_ref, new_base_ref, new_moment_ref):
    for c in range(2):
        total = jnp.sum(got_ref[:, c].astype(jnp.float32), axis=0)
        for j in range(2 * BLOCKS):
            lanes = slice(c * HALF + j * 128, c * HALF + (j + 1) * 128)
            average = total[j * 8:(j + 1) * 8] / N_REP
            moment = MOMENTUM_RATE * moment_ref[:, lanes] + average
            new_moment_ref[:, lanes] = moment
            new_base_ref[:, lanes] = base_ref[:, lanes] - OUTER_RATE * (average + MOMENTUM_RATE * moment)


def outer(got, base, moment):
    shape = jax.ShapeDtypeStruct(base.shape, jnp.float32)
    return pl.pallas_call(
        outer_kernel,
        out_shape=(shape, shape),
        compiler_params=pltpu.CompilerParams(vmem_limit_bytes=8 * 1024 * 1024),
        cost_estimate=COST,
    )(got, base, moment)


def body(activations, cotangent, local_weights, base_shard, momentum):
    x, yhi, c = lax.axis_index("x"), lax.axis_index("yhi"), lax.axis_index("c")
    act, cot, local, base, moment = activations[0], cotangent[0], local_weights[0], base_shard[0], momentum[0]

    def columns(array, start, width):
        return lax.dynamic_slice_in_dim(array, start, width, 1)

    def other_core(array):
        return lax.ppermute(array, "c", shift(2, 1))

    def along_x(array, k):
        return lax.ppermute(array, "x", shift(X, k))

    def all_to_all(array, axes):
        return lax.all_to_all(array, axes, 0, 0, tiled=True)

    def after(array, *others):
        return lax.optimization_barrier((array, *others))[0]

    cot_mine, cot_other = columns(cot, c * HALF, HALF), other_core(columns(cot, (1 - c) * HALF, HALF))

    def group(j, half):
        chunk = slice(j * CHUNK, (j + 1) * CHUNK)

        def packed(k):
            return jnp.stack([columns(act, (half * X + lax.rem(x + k, X)) * ROWS, ROWS), cot_mine[:, chunk], cot_other[:, chunk]])

        return [packed(0)] + [along_x(packed(k), k) for k in range(1, X)]

    def other_features(parts):
        return [other_core(part[0]) for part in parts]

    groups = [group(0, 1 - yhi), group(1, yhi)]
    far_other = other_features(groups[0])
    sent_far = [matmul(far_other, groups[0], groups[0], jnp.bfloat16)]
    groups[1] = after(groups[1], sent_far[0])
    sent_far.append(matmul(far_other, groups[0], groups[1], jnp.bfloat16))
    far = [lax.ppermute(part, "yhi", shift(2, 1)) for part in sent_far]
    near_other = other_features(after(groups[1], sent_far[1]))
    near = [matmul(near_other, groups[1], groups[j], jnp.float32) for j in range(2)]
    far[0] = after(far[0], *near)

    local = after(local, sent_far[1])
    local_mine, local_other = columns(local, c * HALF, HALF), other_core(columns(local, (1 - c) * HALF, HALF))
    local_rows = jnp.concatenate([jnp.where(c == 0, local_mine, local_other), jnp.where(c == 0, local_other, local_mine)])

    sent = base.reshape(8, 2, HALF).transpose(1, 0, 2)
    sent = jnp.broadcast_to(sent[None], (N_REP, 2, 8, HALF)).reshape(2 * N_REP, 8, HALF)
    base_rows = all_to_all(sent, PEERS).reshape(YLO, Z, 2, 8, HALF)

    restored = quantize(near[0], far[0], local_rows, base_rows, 0)
    restored = quantize(near[1], far[1], local_rows, base_rows, 1, restored)
    got = all_to_all(restored.reshape(2 * N_REP, 64, 128), PEERS).reshape(N_REP, 2, 64, 128)
    new_base, new_moment = outer(got, base, moment)
    return new_base[None], new_moment[None]


def solution(mesh):
    fine = Mesh(mesh.devices.reshape(YLO, Z, 2, X, 2), ("ylo", "z", "yhi", "x", "c"))
    rep, fsdp = REP, ("yhi", "x", "c")
    return jax.shard_map(
        body,
        mesh=fine,
        in_specs=(
            P(rep, fsdp, None),
            P(rep, fsdp, None),
            P(rep, fsdp, None),
            P(fsdp, rep, None),
            P(fsdp, rep, None),
        ),
        out_specs=(P(fsdp, rep, None), P(fsdp, rep, None)),
        check_vma=False,
    )
```

```python
import math

import jax
import jax.numpy as jnp
from jax import lax
from jax.experimental import pallas as pl
from jax.experimental.pallas import tpu as pltpu
from jax.sharding import Mesh, PartitionSpec as P

MOMENTUM_RATE = 0.9
OUTER_RATE = 0.7
EPSILON = 1e-06
SINE = (6.57973575592041, -12.987845420837402, 12.207462310791016, -6.687273025512695, 2.36698842048645, -0.5099183320999146)
COST = pl.CostEstimate(flops=1, bytes_accessed=1, transcendentals=0)
REP = ("ylo", "z")
PEERS = ("ylo", "z", "c")
X, YLO, Z = 4, 4, 8
N_REP = YLO * Z
TOK, D, W2 = 192, 4096, 2048
HALF = W2 // 2
CHUNK = HALF // 2
BLOCKS = CHUNK // 128
WIDE = 2
ROWS = 512
INV = 1.0 / math.sqrt(TOK * 16)


def shift(size, k):
    return [(i, (i + k) % size) for i in range(size)]


def matmul_kernel(*refs):
    others, features, columns, out_ref = refs[:X], refs[X:2 * X], refs[2 * X:3 * X], refs[3 * X]
    a_all, c_all, sems = refs[3 * X + 1:]
    copies = []
    for k in range(X):
        copies.append((others[k], a_all.at[k, 1]))
        copies.append((features[k].at[0], a_all.at[k, 0]))
        copies.append((columns[k].at[1:3], c_all.at[k]))
    copies = [pltpu.make_async_copy(*ends, sems.at[i]) for i, ends in enumerate(copies)]
    for copy in copies:
        copy.start()
    for copy in copies:
        copy.wait()
    everything = c_all[...].reshape(2 * X * TOK, CHUNK)
    for m in range(2):
        rows = slice(m * 256, (m + 1) * 256)
        part = lax.dot_general(
            a_all[:, :, :, rows].reshape(2 * X * TOK, 256), everything, (((0,), (0,)), ((), ())),
            preferred_element_type=jnp.float32)
        out_ref[rows, :] = (part * INV).astype(out_ref.dtype)


def matmul(others, features, columns, dtype):
    return pl.pallas_call(
        matmul_kernel,
        out_shape=jax.ShapeDtypeStruct((ROWS, CHUNK), dtype),
        in_specs=[pl.BlockSpec(memory_space=pl.ANY)] * (3 * X),
        out_specs=pl.BlockSpec(memory_space=pltpu.VMEM),
        scratch_shapes=[
            pltpu.VMEM((X, 2, TOK, ROWS), jnp.bfloat16),
            pltpu.VMEM((X, 2, TOK, CHUNK), jnp.bfloat16),
            pltpu.SemaphoreType.DMA((3 * X,)),
        ],
        compiler_params=pltpu.CompilerParams(vmem_limit_bytes=8 * 1024 * 1024),
        cost_estimate=COST,
    )(*others, *features, *columns)


def quantize_kernel(own_ref, part_ref, local_ref, base_ref, out_ref):
    rows = own_ref.shape[0]
    for j in range(0, BLOCKS, 2):
        restored = []
        for col in (j, j + 1):
            lanes = slice(col * 128, (col + 1) * 128)
            gradient = own_ref[:, lanes] + part_ref[:, lanes].astype(jnp.float32)
            base = base_ref[:, :, 0, :, lanes].reshape(rows, 128)
            pseudo = base - (local_ref[:, lanes].astype(jnp.float32) - gradient)
            scale = (jnp.max(jnp.abs(pseudo), axis=1, keepdims=True) + EPSILON).astype(jnp.bfloat16).astype(jnp.float32)
            level = pseudo * (7.0 / scale)
            step = jnp.round(level)
            off = level - step
            square = off * off
            poly = SINE[-1]
            for coef in SINE[-2::-1]:
                poly = poly * square + coef
            code = (step + off * square * poly).astype(jnp.bfloat16).astype(jnp.float32)
            restored.append((code * (scale * (1.0 / 7.0))).reshape(WIDE, Z, 8, 128))
        block = jnp.concatenate(restored, axis=2).astype(jnp.bfloat16)
        out_ref[:, :, 0, j * 8:(j + 2) * 8, :] = block


def quantize(own, part, local, base, chunk, earlier=None):
    steps = YLO // WIDE
    rows = WIDE * 8 * Z
    tile = pl.BlockSpec((rows, CHUNK), lambda c, i: (c * steps + i, 0))
    local_tile = pl.BlockSpec((rows, CHUNK), lambda c, i: (c * steps + i, chunk))
    out_tile = pl.BlockSpec((WIDE, Z, 1, BLOCKS * 8, 128), lambda c, i: (i, 0, c, chunk, 0))
    base_tile = pl.BlockSpec((WIDE, Z, 1, 8, CHUNK), lambda c, i: (i, 0, c, 0, chunk))
    operands, specs, kernel, aliases = [own, part, local, base], [tile, tile, local_tile, base_tile], quantize_kernel, {}
    if earlier is not None:
        operands.append(earlier)
        specs.append(pl.BlockSpec(memory_space=pl.ANY))
        kernel, aliases = (lambda *refs: quantize_kernel(*refs[:4], refs[5])), {4: 0}
    return pl.pallas_call(
        kernel,
        grid=(2, steps),
        out_shape=jax.ShapeDtypeStruct((YLO, Z, 2, 2 * BLOCKS * 8, 128), jnp.bfloat16),
        in_specs=specs,
        out_specs=out_tile,
        input_output_aliases=aliases,
        compiler_params=pltpu.CompilerParams(vmem_limit_bytes=6 * 1024 * 1024),
        cost_estimate=COST,
    )(*operands)


def outer_kernel(got_ref, base_ref, moment_ref, new_base_ref, new_moment_ref):
    for c in range(2):
        total = jnp.sum(got_ref[:, c].astype(jnp.float32), axis=0)
        for j in range(2 * BLOCKS):
            lanes = slice(c * HALF + j * 128, c * HALF + (j + 1) * 128)
            average = total[j * 8:(j + 1) * 8] / N_REP
            moment = MOMENTUM_RATE * moment_ref[:, lanes] + average
            new_moment_ref[:, lanes] = moment
            new_base_ref[:, lanes] = base_ref[:, lanes] - OUTER_RATE * (average + MOMENTUM_RATE * moment)


def outer(got, base, moment):
    shape = jax.ShapeDtypeStruct(base.shape, jnp.float32)
    return pl.pallas_call(
        outer_kernel,
        out_shape=(shape, shape),
        compiler_params=pltpu.CompilerParams(vmem_limit_bytes=8 * 1024 * 1024),
        cost_estimate=COST,
    )(got, base, moment)


def body(activations, cotangent, local_weights, base_shard, momentum):
    x, yhi, c = lax.axis_index("x"), lax.axis_index("yhi"), lax.axis_index("c")
    act, cot, local, base, moment = activations[0], cotangent[0], local_weights[0], base_shard[0], momentum[0]

    def columns(array, start, width):
        return lax.dynamic_slice_in_dim(array, start, width, 1)

    def other_core(array):
        return lax.ppermute(array, "c", shift(2, 1))

    def along_x(array, k):
        return lax.ppermute(array, "x", shift(X, k))

    def all_to_all(array, axes):
        return lax.all_to_all(array, axes, 0, 0, tiled=True)

    def after(array, *others):
        return lax.optimization_barrier((array, *others))[0]

    cot_mine, cot_other = columns(cot, c * HALF, HALF), other_core(columns(cot, (1 - c) * HALF, HALF))

    def group(j, half):
        chunk = slice(j * CHUNK, (j + 1) * CHUNK)

        def packed(k):
            return jnp.stack([columns(act, (half * X + lax.rem(x + k, X)) * ROWS, ROWS), cot_mine[:, chunk], cot_other[:, chunk]])

        return [packed(0)] + [along_x(packed(k), k) for k in range(1, X)]

    def other_features(parts):
        return [other_core(part[0]) for part in parts]

    groups = [group(0, 1 - yhi), group(1, yhi)]
    far_other = other_features(groups[0])
    sent_far = [matmul(far_other, groups[0], groups[0], jnp.bfloat16)]
    groups[1] = after(groups[1], sent_far[0])
    sent_far.append(matmul(far_other, groups[0], groups[1], jnp.bfloat16))
    far = [lax.ppermute(part, "yhi", shift(2, 1)) for part in sent_far]
    near_other = other_features(after(groups[1], sent_far[1]))
    near = [matmul(near_other, groups[1], groups[j], jnp.float32) for j in range(2)]
    far[0] = after(far[0], *near)

    local = after(local, sent_far[1])
    local_mine, local_other = columns(local, c * HALF, HALF), other_core(columns(local, (1 - c) * HALF, HALF))
    local_rows = jnp.concatenate([jnp.where(c == 0, local_mine, local_other), jnp.where(c == 0, local_other, local_mine)])

    sent = base.reshape(8, 2, HALF).transpose(1, 0, 2)
    sent = jnp.broadcast_to(sent[None], (N_REP, 2, 8, HALF)).reshape(2 * N_REP, 8, HALF)
    base_rows = all_to_all(sent, PEERS).reshape(YLO, Z, 2, 8, HALF)

    restored = quantize(near[0], far[0], local_rows, base_rows, 0)
    restored = quantize(near[1], far[1], local_rows, base_rows, 1, restored)
    got = all_to_all(restored.reshape(2 * N_REP, 64, 128), PEERS).reshape(N_REP, 2, 64, 128)
    new_base, new_moment = outer(got, base, moment)
    return new_base[None], new_moment[None]


def solution(mesh):
    fine = Mesh(mesh.devices.reshape(YLO, Z, 2, X, 2), ("ylo", "z", "yhi", "x", "c"))
    rep, fsdp = REP, ("yhi", "x", "c")
    return jax.shard_map(
        body,
        mesh=fine,
        in_specs=(
            P(rep, fsdp, None),
            P(rep, fsdp, None),
            P(rep, fsdp, None),
            P(fsdp, rep, None),
            P(fsdp, rep, None),
        ),
        out_specs=(P(fsdp, rep, None), P(fsdp, rep, None)),
        check_vma=False,
    )
```

```python
import math

import jax
import jax.numpy as jnp
from jax import lax
from jax.experimental import pallas as pl
from jax.experimental.pallas import tpu as pltpu
from jax.sharding import Mesh, PartitionSpec as P

MOMENTUM_RATE = 0.9
OUTER_RATE = 0.7
EPSILON = 1e-06
SINE = (6.57973575592041, -12.987845420837402, 12.207462310791016, -6.687273025512695, 2.36698842048645, -0.5099183320999146)
COST = pl.CostEstimate(flops=1, bytes_accessed=1, transcendentals=0)
REP = ("ylo", "z")
PEERS = ("ylo", "z", "c")
X, YLO, Z = 4, 4, 8
N_REP = YLO * Z
TOK, D, W2 = 192, 4096, 2048
HALF = W2 // 2
CHUNK = HALF // 2
BLOCKS = CHUNK // 128
WIDE = 2
ROWS = 512
INV = 1.0 / math.sqrt(TOK * 16)


def shift(size, k):
    return [(i, (i + k) % size) for i in range(size)]


def matmul_kernel(*refs):
    others, features, columns, out_ref = refs[:X], refs[X:2 * X], refs[2 * X:3 * X], refs[3 * X]
    everything = jnp.concatenate([part for ref in columns for part in (ref[1], ref[2])])
    for m in range(2):
        rows = slice(m * 256, (m + 1) * 256)
        tokens = jnp.concatenate([part for k in range(X) for part in (features[k][0, :, rows], others[k][:, rows])])
        part = lax.dot_general(tokens, everything, (((0,), (0,)), ((), ())), preferred_element_type=jnp.float32)
        out_ref[rows, :] = (part * INV).astype(out_ref.dtype)


def matmul(others, features, columns, dtype):
    return pl.pallas_call(
        matmul_kernel,
        out_shape=jax.ShapeDtypeStruct((ROWS, CHUNK), dtype),
        in_specs=[pl.BlockSpec(memory_space=pltpu.VMEM)] * (3 * X),
        out_specs=pl.BlockSpec(memory_space=pltpu.VMEM),
        compiler_params=pltpu.CompilerParams(vmem_limit_bytes=14 * 1024 * 1024),
        cost_estimate=COST,
    )(*others, *features, *columns)


def quantize_kernel(own_ref, part_ref, local_ref, base_ref, out_ref):
    rows = own_ref.shape[0]
    for j in range(0, BLOCKS, 2):
        restored = []
        for col in (j, j + 1):
            lanes = slice(col * 128, (col + 1) * 128)
            gradient = own_ref[:, lanes] + part_ref[:, lanes].astype(jnp.float32)
            base = base_ref[:, :, 0, :, lanes].reshape(rows, 128)
            pseudo = base - (local_ref[:, lanes].astype(jnp.float32) - gradient)
            scale = (jnp.max(jnp.abs(pseudo), axis=1, keepdims=True) + EPSILON).astype(jnp.bfloat16).astype(jnp.float32)
            level = pseudo * (7.0 / scale)
            step = jnp.round(level)
            off = level - step
            square = off * off
            poly = SINE[-1]
            for coef in SINE[-2::-1]:
                poly = poly * square + coef
            code = (step + off * square * poly).astype(jnp.bfloat16).astype(jnp.float32)
            restored.append((code * (scale * (1.0 / 7.0))).reshape(WIDE, Z, 8, 128))
        block = jnp.concatenate(restored, axis=2).astype(jnp.bfloat16)
        out_ref[:, :, 0, j * 8:(j + 2) * 8, :] = block


def quantize(own, part, local, base, chunk, earlier=None):
    steps = YLO // WIDE
    rows = WIDE * 8 * Z
    tile = pl.BlockSpec((rows, CHUNK), lambda c, i: (c * steps + i, 0))
    local_tile = pl.BlockSpec((rows, CHUNK), lambda c, i: (c * steps + i, chunk))
    out_tile = pl.BlockSpec((WIDE, Z, 1, BLOCKS * 8, 128), lambda c, i: (i, 0, c, chunk, 0))
    base_tile = pl.BlockSpec((WIDE, Z, 1, 8, CHUNK), lambda c, i: (i, 0, c, 0, chunk))
    operands, specs, kernel, aliases = [own, part, local, base], [tile, tile, local_tile, base_tile], quantize_kernel, {}
    if earlier is not None:
        operands.append(earlier)
        specs.append(pl.BlockSpec(memory_space=pl.ANY))
        kernel, aliases = (lambda *refs: quantize_kernel(*refs[:4], refs[5])), {4: 0}
    return pl.pallas_call(
        kernel,
        grid=(2, steps),
        out_shape=jax.ShapeDtypeStruct((YLO, Z, 2, 2 * BLOCKS * 8, 128), jnp.bfloat16),
        in_specs=specs,
        out_specs=out_tile,
        input_output_aliases=aliases,
        compiler_params=pltpu.CompilerParams(vmem_limit_bytes=6 * 1024 * 1024),
        cost_estimate=COST,
    )(*operands)


def outer_kernel(got_ref, base_ref, moment_ref, new_base_ref, new_moment_ref):
    for c in range(2):
        total = jnp.sum(got_ref[:, c].astype(jnp.float32), axis=0)
        for j in range(2 * BLOCKS):
            lanes = slice(c * HALF + j * 128, c * HALF + (j + 1) * 128)
            average = total[j * 8:(j + 1) * 8] / N_REP
            moment = MOMENTUM_RATE * moment_ref[:, lanes] + average
            new_moment_ref[:, lanes] = moment
            new_base_ref[:, lanes] = base_ref[:, lanes] - OUTER_RATE * (average + MOMENTUM_RATE * moment)


def outer(got, base, moment):
    shape = jax.ShapeDtypeStruct(base.shape, jnp.float32)
    return pl.pallas_call(
        outer_kernel,
        out_shape=(shape, shape),
        compiler_params=pltpu.CompilerParams(vmem_limit_bytes=8 * 1024 * 1024),
        cost_estimate=COST,
    )(got, base, moment)


def body(activations, cotangent, local_weights, base_shard, momentum):
    x, yhi, c = lax.axis_index("x"), lax.axis_index("yhi"), lax.axis_index("c")
    act, cot, local, base, moment = activations[0], cotangent[0], local_weights[0], base_shard[0], momentum[0]

    def columns(array, start, width):
        return lax.dynamic_slice_in_dim(array, start, width, 1)

    def other_core(array):
        return lax.ppermute(array, "c", shift(2, 1))

    def along_x(array, k):
        return lax.ppermute(array, "x", shift(X, k))

    def all_to_all(array, axes):
        return lax.all_to_all(array, axes, 0, 0, tiled=True)

    def after(array, *others):
        return lax.optimization_barrier((array, *others))[0]

    cot_mine, cot_other = columns(cot, c * HALF, HALF), other_core(columns(cot, (1 - c) * HALF, HALF))

    def group(j, half):
        chunk = slice(j * CHUNK, (j + 1) * CHUNK)

        def packed(k):
            return jnp.stack([columns(act, (half * X + lax.rem(x + k, X)) * ROWS, ROWS), cot_mine[:, chunk], cot_other[:, chunk]])

        return [packed(0)] + [along_x(packed(k), k) for k in range(1, X)]

    def other_features(parts):
        return [other_core(part[0]) for part in parts]

    groups = [group(0, 1 - yhi), group(1, yhi)]
    far_other = other_features(groups[0])
    sent_far = [matmul(far_other, groups[0], groups[0], jnp.bfloat16)]
    groups[1] = after(groups[1], sent_far[0])
    sent_far.append(matmul(far_other, groups[0], groups[1], jnp.bfloat16))
    far = [lax.ppermute(part, "yhi", shift(2, 1)) for part in sent_far]
    near_other = other_features(after(groups[1], sent_far[1]))
    near = [matmul(near_other, groups[1], groups[j], jnp.float32) for j in range(2)]
    far[0] = after(far[0], *near)

    local = after(local, sent_far[1])
    local_mine, local_other = columns(local, c * HALF, HALF), other_core(columns(local, (1 - c) * HALF, HALF))
    local_rows = jnp.concatenate([jnp.where(c == 0, local_mine, local_other), jnp.where(c == 0, local_other, local_mine)])

    sent = base.reshape(8, 2, HALF).transpose(1, 0, 2)
    sent = jnp.broadcast_to(sent[None], (N_REP, 2, 8, HALF)).reshape(2 * N_REP, 8, HALF)
    base_rows = all_to_all(sent, PEERS).reshape(YLO, Z, 2, 8, HALF)

    restored = quantize(near[0], far[0], local_rows, base_rows, 0)
    restored = quantize(near[1], far[1], local_rows, base_rows, 1, restored)
    got = all_to_all(restored.reshape(2 * N_REP, 64, 128), PEERS).reshape(N_REP, 2, 64, 128)
    new_base, new_moment = outer(got, base, moment)
    return new_base[None], new_moment[None]


def solution(mesh):
    fine = Mesh(mesh.devices.reshape(YLO, Z, 2, X, 2), ("ylo", "z", "yhi", "x", "c"))
    rep, fsdp = REP, ("yhi", "x", "c")
    return jax.shard_map(
        body,
        mesh=fine,
        in_specs=(
            P(rep, fsdp, None),
            P(rep, fsdp, None),
            P(rep, fsdp, None),
            P(fsdp, rep, None),
            P(fsdp, rep, None),
        ),
        out_specs=(P(fsdp, rep, None), P(fsdp, rep, None)),
        check_vma=False,
    )
```

```python
import math

import jax
import jax.numpy as jnp
from jax import lax
from jax.experimental import pallas as pl
from jax.experimental.pallas import tpu as pltpu
from jax.sharding import Mesh, PartitionSpec as P

MOMENTUM_RATE = 0.9
OUTER_RATE = 0.7
EPSILON = 1e-06
SINE = (6.57973575592041, -12.987845420837402, 12.207462310791016, -6.687273025512695, 2.36698842048645, -0.5099183320999146)
COST = pl.CostEstimate(flops=1, bytes_accessed=1, transcendentals=0)
REP = ("ylo", "z")
PEERS = ("ylo", "z", "c")
X, YLO, Z = 4, 4, 8
N_REP = YLO * Z
TOK, D, W2 = 192, 4096, 2048
HALF = W2 // 2
CHUNK = HALF // 2
BLOCKS = CHUNK // 128
WIDE = 4
ROWS = 512
INV = 1.0 / math.sqrt(TOK * 16)


def shift(size, k):
    return [(i, (i + k) % size) for i in range(size)]


def matmul_kernel(*refs):
    others, features, columns, out_ref = refs[:X], refs[X:2 * X], refs[2 * X:3 * X], refs[3 * X]
    everything = jnp.concatenate([part for ref in columns for part in (ref[1], ref[2])])
    for m in range(2):
        rows = slice(m * 256, (m + 1) * 256)
        tokens = jnp.concatenate([part for k in range(X) for part in (features[k][0, :, rows], others[k][:, rows])])
        part = lax.dot_general(tokens, everything, (((0,), (0,)), ((), ())), preferred_element_type=jnp.float32)
        out_ref[rows, :] = (part * INV).astype(out_ref.dtype)


def matmul(others, features, columns, dtype):
    return pl.pallas_call(
        matmul_kernel,
        out_shape=jax.ShapeDtypeStruct((ROWS, CHUNK), dtype),
        in_specs=[pl.BlockSpec(memory_space=pltpu.VMEM)] * (3 * X),
        out_specs=pl.BlockSpec(memory_space=pltpu.VMEM),
        compiler_params=pltpu.CompilerParams(vmem_limit_bytes=14 * 1024 * 1024),
        cost_estimate=COST,
    )(*others, *features, *columns)


def quantize_kernel(own_ref, part_ref, local_ref, base_ref, out_ref):
    rows = own_ref.shape[0]
    for j in range(0, BLOCKS, 2):
        restored = []
        for col in (j, j + 1):
            lanes = slice(col * 128, (col + 1) * 128)
            gradient = own_ref[:, lanes] + part_ref[:, lanes].astype(jnp.float32)
            base = base_ref[:, :, 0, :, lanes].reshape(rows, 128)
            pseudo = base - (local_ref[:, lanes].astype(jnp.float32) - gradient)
            scale = (jnp.max(jnp.abs(pseudo), axis=1, keepdims=True) + EPSILON).astype(jnp.bfloat16).astype(jnp.float32)
            level = pseudo * (7.0 / scale)
            step = jnp.round(level)
            off = level - step
            square = off * off
            poly = SINE[-1]
            for coef in SINE[-2::-1]:
                poly = poly * square + coef
            code = (step + off * square * poly).astype(jnp.bfloat16).astype(jnp.float32)
            restored.append((code * (scale * (1.0 / 7.0))).reshape(WIDE, Z, 8, 128))
        block = jnp.concatenate(restored, axis=2).astype(jnp.bfloat16)
        out_ref[:, :, 0, j * 8:(j + 2) * 8, :] = block


def quantize(own, part, local, base, chunk, earlier=None):
    steps = YLO // WIDE
    rows = WIDE * 8 * Z
    tile = pl.BlockSpec((rows, CHUNK), lambda c, i: (c * steps + i, 0))
    local_tile = pl.BlockSpec((rows, CHUNK), lambda c, i: (c * steps + i, chunk))
    out_tile = pl.BlockSpec((WIDE, Z, 1, BLOCKS * 8, 128), lambda c, i: (i, 0, c, chunk, 0))
    base_tile = pl.BlockSpec((WIDE, Z, 1, 8, CHUNK), lambda c, i: (i, 0, c, 0, chunk))
    operands, specs, kernel, aliases = [own, part, local, base], [tile, tile, local_tile, base_tile], quantize_kernel, {}
    if earlier is not None:
        operands.append(earlier)
        specs.append(pl.BlockSpec(memory_space=pl.ANY))
        kernel, aliases = (lambda *refs: quantize_kernel(*refs[:4], refs[5])), {4: 0}
    return pl.pallas_call(
        kernel,
        grid=(2, steps),
        out_shape=jax.ShapeDtypeStruct((YLO, Z, 2, 2 * BLOCKS * 8, 128), jnp.bfloat16),
        in_specs=specs,
        out_specs=out_tile,
        input_output_aliases=aliases,
        compiler_params=pltpu.CompilerParams(vmem_limit_bytes=10 * 1024 * 1024),
        cost_estimate=COST,
    )(*operands)


def outer_kernel(got_ref, base_ref, moment_ref, new_base_ref, new_moment_ref):
    for c in range(2):
        total = jnp.sum(got_ref[:, c].astype(jnp.float32), axis=0)
        for j in range(2 * BLOCKS):
            lanes = slice(c * HALF + j * 128, c * HALF + (j + 1) * 128)
            average = total[j * 8:(j + 1) * 8] / N_REP
            moment = MOMENTUM_RATE * moment_ref[:, lanes] + average
            new_moment_ref[:, lanes] = moment
            new_base_ref[:, lanes] = base_ref[:, lanes] - OUTER_RATE * (average + MOMENTUM_RATE * moment)


def outer(got, base, moment):
    shape = jax.ShapeDtypeStruct(base.shape, jnp.float32)
    return pl.pallas_call(
        outer_kernel,
        out_shape=(shape, shape),
        compiler_params=pltpu.CompilerParams(vmem_limit_bytes=8 * 1024 * 1024),
        cost_estimate=COST,
    )(got, base, moment)


def body(activations, cotangent, local_weights, base_shard, momentum):
    x, yhi, c = lax.axis_index("x"), lax.axis_index("yhi"), lax.axis_index("c")
    act, cot, local, base, moment = activations[0], cotangent[0], local_weights[0], base_shard[0], momentum[0]

    def columns(array, start, width):
        return lax.dynamic_slice_in_dim(array, start, width, 1)

    def other_core(array):
        return lax.ppermute(array, "c", shift(2, 1))

    def along_x(array, k):
        return lax.ppermute(array, "x", shift(X, k))

    def all_to_all(array, axes):
        return lax.all_to_all(array, axes, 0, 0, tiled=True)

    def after(array, *others):
        return lax.optimization_barrier((array, *others))[0]

    cot_mine, cot_other = columns(cot, c * HALF, HALF), other_core(columns(cot, (1 - c) * HALF, HALF))

    def group(j, half):
        chunk = slice(j * CHUNK, (j + 1) * CHUNK)

        def packed(k):
            return jnp.stack([columns(act, (half * X + lax.rem(x + k, X)) * ROWS, ROWS), cot_mine[:, chunk], cot_other[:, chunk]])

        return [packed(0)] + [along_x(packed(k), k) for k in range(1, X)]

    def other_features(parts):
        return [other_core(part[0]) for part in parts]

    groups = [group(0, 1 - yhi), group(1, yhi)]
    far_other = other_features(groups[0])
    sent_far = [matmul(far_other, groups[0], groups[0], jnp.bfloat16)]
    groups[1] = after(groups[1], sent_far[0])
    sent_far.append(matmul(far_other, groups[0], groups[1], jnp.bfloat16))
    far = [lax.ppermute(part, "yhi", shift(2, 1)) for part in sent_far]
    near_other = other_features(after(groups[1], sent_far[1]))
    near = [matmul(near_other, groups[1], groups[j], jnp.float32) for j in range(2)]
    far[0] = after(far[0], *near)

    local = after(local, sent_far[1])
    local_mine, local_other = columns(local, c * HALF, HALF), other_core(columns(local, (1 - c) * HALF, HALF))
    local_rows = jnp.concatenate([jnp.where(c == 0, local_mine, local_other), jnp.where(c == 0, local_other, local_mine)])

    sent = base.reshape(8, 2, HALF).transpose(1, 0, 2)
    sent = jnp.broadcast_to(sent[None], (N_REP, 2, 8, HALF)).reshape(2 * N_REP, 8, HALF)
    base_rows = all_to_all(sent, PEERS).reshape(YLO, Z, 2, 8, HALF)

    restored = quantize(near[0], far[0], local_rows, base_rows, 0)
    restored = quantize(near[1], far[1], local_rows, base_rows, 1, restored)
    got = all_to_all(restored.reshape(2 * N_REP, 64, 128), PEERS).reshape(N_REP, 2, 64, 128)
    new_base, new_moment = outer(got, base, moment)
    return new_base[None], new_moment[None]


def solution(mesh):
    fine = Mesh(mesh.devices.reshape(YLO, Z, 2, X, 2), ("ylo", "z", "yhi", "x", "c"))
    rep, fsdp = REP, ("yhi", "x", "c")
    return jax.shard_map(
        body,
        mesh=fine,
        in_specs=(
            P(rep, fsdp, None),
            P(rep, fsdp, None),
            P(rep, fsdp, None),
            P(fsdp, rep, None),
            P(fsdp, rep, None),
        ),
        out_specs=(P(fsdp, rep, None), P(fsdp, rep, None)),
        check_vma=False,
    )
```
